32 devices in a mesh: region: 16 (over z, y, core), tracer: 2 (over x).
Axes of the slice: x: 2, y: 2, z: 4, core: 2. Of those that a mesh axis runs over, the one named last changes fastest.
Arguments:
- cotangent: float32 [32, 8192], P('tracer', 'region'), may hold values from -6 to 6
- states: float32 [6, 32, 8192], P(None, 'tracer', 'region'), may hold values from -6 to 6
- implicit_inverse: float32 [256, 32, 32], P('region'), may hold values from -3 to 3
- wet_levels: int32 [256], P('region'), may hold values from 1 to 32
- explicit_tiles: bfloat16 [16, 5, 512, 512], P('region'), may hold values from -0.125 to 0.125
- tile_offset: int32 [16, 5], P('region'), may hold values from -2 to 2, as said below
- tile_count: int32 [16], P('region'), may hold values from 1 to 5
- uptake_weight: float32 [32, 32], replicated, may hold values from -1 to 1
- release_weight: float32 [32, 32], replicated, may hold values from -1 to 1
Outputs:
- initial_adjoint: float32 [32, 8192], P('tracer', 'region')
The draws below stay inside these ranges and needn't reach their ends.
Inputs may be any that keep to these rules, and one draw needn't show every extreme that they name: `tile_offset`: the offsets of one region are distinct; only the first tile_count slots of a region are used.
All inputs are finite; a program needn't handle non-finite values.
Results may differ from the reference program's by a relative error of at most 0.0032.
Values sent between devices are 32-bit elements; how exact they have to be, the bound alone decides.
A program may use at most 64 MiB of HBM per device.

```python
import math
import jax
import jax.numpy as jnp
from jax import lax

NTR = 32
LEV = 32
STEPS = 6
REACH = 2
TILES = 5
BOX_DEV = 512
REGIONS = 16
BOXES = 8192
NCOL = 256


def draw_implicit_inverse(key, part):
    noise = jax.random.normal(key, (NCOL, LEV, LEV), jnp.float32)
    identity = jnp.eye(LEV, dtype=jnp.float32)
    return jnp.clip(identity[None] + 0.5 * noise / math.sqrt(LEV), -3.0, 3.0)


def one_order(subkey):
    return jax.random.permutation(subkey, TILES)


def draw_tile_offset(key, part):
    subkeys = jax.random.split(jax.random.fold_in(key, 17), REGIONS)
    return (jax.vmap(one_order)(subkeys).astype(jnp.int32) - REACH).astype(jnp.int32)


def with_ends(entries, rng, smallest, top_value):
    extent = entries.shape
    place = [jax.random.randint(jax.random.fold_in(rng, axis), (), 0, extent[axis]) for axis in range(len(extent))]
    entries = entries.at[tuple(place)].set(smallest)
    longest = extent.index(max(extent))
    place[longest] = (place[longest] + 1) % extent[longest]
    return entries.at[tuple(place)].set(top_value)


def steps_of(own_key, dims, pieces, low, largest):
    level, own = 1.0, jax.random.fold_in(own_key, 6)
    for dim, shards_of in pieces:
        steps = jnp.exp(jax.random.uniform(jax.random.fold_in(own, dim), (shards_of,), jnp.float32, low / len(pieces), largest / len(pieces)))
        level = level * jnp.repeat(steps, dims[dim] // shards_of).reshape([-1 if axis == dim else 1 for axis in range(len(dims))])
    return level


def normal_values(key, dims, spread, reach, shards=(), held_as=jnp.bfloat16):
    level = steps_of(key, dims, shards, -0.22, 0.18) if shards else 1.0
    result = jax.random.normal(key, dims, jnp.float32) * spread * level
    return jnp.minimum(jnp.maximum(result, -reach), reach).astype(held_as)


def setup_inputs(seed: int = 0) -> dict:
    seeds = jax.random.split(jax.random.key(seed), 10)
    return {
        "cotangent": normal_values(seeds[0], (NTR, BOXES), 1.0, 6.0, ((0, 2), (1, 16)), jnp.float32),
        "states": normal_values(seeds[1], (STEPS, NTR, BOXES), 1.0, 6.0, ((1, 2), (2, 16)), jnp.float32),
        "implicit_inverse": draw_implicit_inverse(jax.random.fold_in(seeds[9], 71), 0),
        "wet_levels": with_ends(jax.random.randint(seeds[3], (NCOL,), 1, LEV + 1), jax.random.fold_in(seeds[3], 1), 1, LEV).astype(jnp.int32),
        "explicit_tiles": normal_values(seeds[4], (REGIONS, TILES, BOX_DEV, BOX_DEV), (4 * BOX_DEV) ** -0.5, 0.125, ((0, 16),)),
        "tile_offset": draw_tile_offset(jax.random.fold_in(seeds[9], 71), 0),
        "tile_count": with_ends(jax.random.randint(seeds[6], (REGIONS,), 1, TILES + 1), jax.random.fold_in(seeds[6], 1), 1, TILES).astype(jnp.int32),
        "uptake_weight": normal_values(seeds[7], (NTR, NTR), NTR ** -0.5, 1.0, (), jnp.float32),
        "release_weight": normal_values(seeds[8], (NTR, NTR), NTR ** -0.5, 1.0, (), jnp.float32),
    }


def region_terms(paired):
    region_block, tile_block = paired
    return jnp.einsum('tb,kbc->ktc', region_block.astype(jnp.float32), tile_block.astype(jnp.float32), precision=lax.Precision.HIGHEST)


def reference(cotangent, states, implicit_inverse, wet_levels, explicit_tiles, tile_offset, tile_count, uptake_weight, release_weight):
    highest = lax.Precision.HIGHEST
    wet_mask = (jnp.arange(LEV, dtype=jnp.int32)[None, :] < wet_levels[:, None]).astype(jnp.float32).reshape(1, BOXES)
    live_slots = (jnp.arange(TILES, dtype=jnp.int32)[None, :] < tile_count[:, None]).astype(jnp.float32)
    targets = ((jnp.arange(REGIONS, dtype=jnp.int32)[:, None] + tile_offset) % REGIONS).astype(jnp.int32)
    adjoint = cotangent
    for section in range(STEPS - 1, -1, -1):
        columns = adjoint.reshape(NTR, NCOL, LEV)
        settled = jnp.einsum('tcm,cml->tcl', columns, implicit_inverse, precision=highest).reshape(NTR, BOXES) * wet_mask
        settled_half = settled.astype(jnp.bfloat16)
        by_region = settled_half.reshape(NTR, REGIONS, BOX_DEV).transpose(1, 0, 2)
        terms = lax.map(region_terms, (by_region, explicit_tiles))
        terms = terms * live_slots[:, :, None, None]
        inflow = jnp.zeros((REGIONS, NTR, BOX_DEV), jnp.float32)
        inflow = inflow.at[targets.reshape(-1)].add(terms.reshape(REGIONS * TILES, NTR, BOX_DEV))
        inflow = inflow.transpose(1, 0, 2).reshape(NTR, BOXES)
        uptake = jnp.dot(uptake_weight, states[section], precision=highest)
        pushed = jnp.dot(release_weight.T, settled, precision=highest)
        reacted = jnp.dot(uptake_weight.T, (1.0 - jnp.tanh(uptake) ** 2) * pushed, precision=highest)
        adjoint = wet_mask * (inflow + reacted)
    return adjoint
```

```python
import functools

import jax
import jax.numpy as jnp
from jax import lax
from jax.experimental import pallas as pl
from jax.experimental.pallas import tpu as pltpu
from jax.sharding import PartitionSpec as P

MESH = pl.DeviceIdType.MESH
F32, BF16 = jnp.float32, jnp.bfloat16
LANES = 128
ROWS_DIM = (((1,), (1,)), ((), ()))


def halves(x):
    high = x.astype(BF16)
    return high, (x - high.astype(F32)).astype(BF16)


def dot(a, b):
    return jnp.dot(a, b, preferred_element_type=F32)


def dot_split(a, b):
    (a_high, a_low), (b_high, b_low) = a, halves(b)
    return dot(a_high, b_high) + (dot(a_high, b_low) + dot(a_low, b_high))


def kernel(
    cot_hbm, states_hbm, inv_hbm, wet, tiles_hbm, off, cnt, up_hbm, rel_hbm,
    out,
    tiles, inv, up, rel, adj, full_state, full_settled, gain,
    relay_out, direct_out, peer_out, merged_out,
    relay_in, direct_in, peer_in, merged_in,
    load_sem, own_sem, send_sem, recv_sem, settled_send, settled_recv, state_send, state_recv,
):
    steps, tracers_n, tr, boxes = full_state.shape
    columns, levels, _ = inv.shape
    slots = tiles.shape[0]
    ntr = tracers_n * tr
    region, tracer = lax.axis_index("region"), lax.axis_index("tracer")
    regions = lax.axis_size("region")

    sign = 2 * lax.rem(region, 2) - 1
    at = lambda distance: lax.rem(region + distance * sign + 2 * regions, regions)
    inner, outer, far, behind = at(-1), at(1), at(2), at(-2)
    others = [lax.rem(tracer + j, tracers_n) for j in range(1, tracers_n)]

    loads = [
        pltpu.make_async_copy(src, dst, load_sem.at[k])
        for k, (src, dst) in enumerate(
            [(inv_hbm, inv), (cot_hbm, adj), (up_hbm, up), (rel_hbm, rel), (tiles_hbm.at[0], tiles)]
        )
    ]
    for load in loads:
        load.start()
    own_states = [
        pltpu.make_async_copy(states_hbm.at[n], full_state.at[n, tracer], own_sem.at[n])
        for n in range(steps)
    ]
    for copy in own_states[::-1]:
        copy.start()

    barrier = pltpu.get_barrier_semaphore()
    for device in (inner, outer, behind):
        pl.semaphore_signal(barrier, inc=1, device_id={"region": device}, device_id_type=MESH)
    for other in others:
        pl.semaphore_signal(barrier, inc=1, device_id={"tracer": other}, device_id_type=MESH)
    pl.semaphore_wait(barrier, 3 + len(others))

    def state_copy(n, j):
        return pltpu.make_async_remote_copy(
            src_ref=states_hbm.at[n],
            dst_ref=full_state.at[n, tracer],
            send_sem=state_send.at[n, j],
            recv_sem=state_recv.at[n, j],
            device_id={"tracer": others[j]},
            device_id_type=MESH,
        )

    def settled_copy(i, j):
        return pltpu.make_async_remote_copy(
            src_ref=full_settled.at[i, tracer],
            dst_ref=full_settled.at[i, tracer],
            send_sem=settled_send.at[i, j],
            recv_sem=settled_recv.at[i, j],
            device_id={"tracer": others[j]},
            device_id_type=MESH,
        )

    def region_copy(i, k):
        src, dst, target = (
            (relay_out, relay_in, inner),
            (direct_out, direct_in, far),
            (peer_out, peer_in, inner),
            (merged_out, merged_in, outer),
        )[k]
        return pltpu.make_async_remote_copy(
            src_ref=src.at[i],
            dst_ref=dst.at[i],
            send_sem=send_sem.at[i, k],
            recv_sem=recv_sem.at[i, k],
            device_id={"region": target},
            device_id_type=MESH,
        )

    peers = range(len(others))
    for n in range(steps - 1, max(steps - 3, -1), -1):
        for j in peers:
            state_copy(n, j).start()

    lane = lax.broadcasted_iota(jnp.int32, (1, boxes), 1)
    wet_of = jnp.zeros((1, boxes), jnp.int32)
    for c in range(columns):
        wet_of = jnp.where(lane // levels == c, wet[c], wet_of)
    wet_mask = (lane % levels < wet_of).astype(F32)

    def tile_at(distance):
        slot, live = jnp.int32(0), jnp.int32(0)
        for k in range(slots):
            hit = jnp.logical_and(off[0, k] == distance * sign, k < cnt[0])
            slot = jnp.where(hit, k, slot)
            live = jnp.where(hit, 1, live)
        return slot, live.astype(F32)

    places = {d: tile_at(d) for d in (-2, 2, -1, 1, 0)}

    for load in loads[:4]:
        load.wait()
    per = LANES // levels
    flat = inv[...].reshape(boxes, levels)
    wide = jnp.concatenate([flat] * per, axis=1)
    row = lax.broadcasted_iota(jnp.int32, (boxes, LANES), 0)
    lanes = lax.broadcasted_iota(jnp.int32, (boxes, LANES), 1)
    wide = jnp.where((row // levels) % per == lanes // levels, wide, 0.0)
    blocks = []
    for b in range(boxes // LANES):
        span = slice(b * LANES, (b + 1) * LANES)
        high, low = halves(wide[span] * wet_mask[:, span])
        blocks.append(jnp.concatenate([high, low], axis=0))

    ident = (
        lax.broadcasted_iota(jnp.int32, (ntr, ntr), 0) == lax.broadcasted_iota(jnp.int32, (ntr, ntr), 1)
    ).astype(F32)
    own_rows = (
        lax.broadcasted_iota(jnp.int32, (tr, ntr), 0) + tracer * tr
        == lax.broadcasted_iota(jnp.int32, (tr, ntr), 1)
    ).astype(F32)
    highest = lax.Precision.HIGHEST
    uptake = halves(up[...])
    uptake_own = halves(
        lax.dot_general(own_rows, up[...], ROWS_DIM, precision=highest, preferred_element_type=F32)
    )
    release = halves(
        lax.dot_general(ident, rel[...], ROWS_DIM, precision=highest, preferred_element_type=F32)
    )

    def joined(ref, i):
        if tr % 8 == 0:
            return ref[i].reshape(ntr, boxes)
        return jnp.concatenate([ref[i, j] for j in range(tracers_n)], axis=0)

    def settle(a):
        high, low = halves(a)
        zero = jnp.zeros((tr, LANES), BF16)
        parts = []
        for b, block in enumerate(blocks):
            span = slice(b * LANES, (b + 1) * LANES)
            first = jnp.concatenate([high[:, span], high[:, span]], axis=1)
            second = jnp.concatenate([low[:, span], zero], axis=1)
            if tr % 16 == 0:
                both = dot(jnp.concatenate([first, second], axis=0), block)
                parts.append(both[:tr] + both[tr:])
            else:
                parts.append(dot(first, block) + dot(second, block))
        return jnp.concatenate(parts, axis=1)

    def make_gain(n):
        for j in peers:
            state_copy(n, j).wait_recv()
        pltpu.make_async_copy(states_hbm.at[n], full_state.at[n, tracer], own_sem.at[n]).wait()
        bent = jnp.tanh(dot_split(uptake, joined(full_state, n)))
        gain[...] = 1.0 - bent * bent

    def step(i, carry):
        n = steps - 1 - i
        settled = settle(adj[...])
        full_settled[i, tracer] = settled
        for j in peers:
            settled_copy(i, j).start()
        half = settled.astype(BF16)

        @pl.when(i == 0)
        def _():
            loads[4].wait()

        def term(distance):
            slot, live = places[distance]
            return dot(half, tiles[slot]) * live

        relay_out[i] = term(-2)
        region_copy(i, 0).start()
        direct_out[i] = term(2)
        region_copy(i, 1).start()
        near = term(1)
        region_copy(i, 0).wait_recv()
        merged_out[i] = near + relay_in[i]
        region_copy(i, 3).start()
        peer_out[i] = term(-1)
        region_copy(i, 2).start()

        @pl.when(n >= 2)
        def _():
            for j in peers:
                state_copy(n - 2, j).start()

        total = term(0)

        @pl.when(i == 0)
        def _():
            make_gain(n)

        for j in peers:
            settled_copy(i, j).wait_recv()
        weighted = gain[...] * dot_split(release, joined(full_settled, i))
        total = total + dot_split(uptake_own, weighted)

        @pl.when(n >= 1)
        def _():
            make_gain(n - 1)

        region_copy(i, 2).wait_recv()
        total = total + peer_in[i]
        region_copy(i, 1).wait_recv()
        total = total + direct_in[i]
        region_copy(i, 3).wait_recv()
        adj[...] = wet_mask * (total + merged_in[i])
        return carry

    lax.fori_loop(0, steps, step, 0)
    out[...] = adj[...]

    def drain(i, carry):
        for k in range(4):
            region_copy(i, k).wait_send()
        for j in peers:
            settled_copy(i, j).wait_send()
            state_copy(i, j).wait_send()
        return carry

    lax.fori_loop(0, steps, drain, 0)


def local(
    cotangent,
    states,
    implicit_inverse,
    wet_levels,
    explicit_tiles,
    tile_offset,
    tile_count,
    uptake_weight,
    release_weight,
):
    tr, boxes = cotangent.shape
    steps = states.shape[0]
    tracers_n = lax.axis_size("tracer")
    ntr = tracers_n * tr
    slots = explicit_tiles.shape[1]
    peers = max(tracers_n - 1, 1)
    hbm = pl.BlockSpec(memory_space=pl.ANY)
    smem = pl.BlockSpec(memory_space=pltpu.SMEM)
    message = pltpu.VMEM((steps, tr, boxes), F32)
    gathered = pltpu.VMEM((steps, tracers_n, tr, boxes), F32)
    sems = pltpu.SemaphoreType.DMA
    return pl.pallas_call(
        kernel,
        out_shape=jax.ShapeDtypeStruct((tr, boxes), F32),
        in_specs=[hbm, hbm, hbm, smem, hbm, smem, smem, hbm, hbm],
        out_specs=pl.BlockSpec(memory_space=pltpu.VMEM),
        scratch_shapes=[
            pltpu.VMEM(explicit_tiles.shape[1:], BF16),
            pltpu.VMEM(implicit_inverse.shape, F32),
            pltpu.VMEM(uptake_weight.shape, F32),
            pltpu.VMEM(release_weight.shape, F32),
            pltpu.VMEM((tr, boxes), F32),
            gathered,
            gathered,
            pltpu.VMEM((ntr, boxes), F32),
        ]
        + [message] * 8
        + [
            sems((5,)),
            sems((steps,)),
            sems((steps, 4)),
            sems((steps, 4)),
            sems((steps, peers)),
            sems((steps, peers)),
            sems((steps, peers)),
            sems((steps, peers)),
        ],
        compiler_params=pltpu.CompilerParams(
            collective_id=0, has_side_effects=True, vmem_limit_bytes=40 * 1024 * 1024
        ),
        name="adjoint_steps",
    )(
        cotangent,
        states,
        implicit_inverse,
        wet_levels,
        explicit_tiles,
        tile_offset,
        tile_count,
        uptake_weight,
        release_weight,
    )


def solution(mesh):
    placed = (
        P("tracer", "region"),
        P(None, "tracer", "region"),
        P("region", None, None),
        P("region"),
        P("region", None, None, None),
        P("region", None),
        P("region"),
        P(),
        P(),
    )
    return jax.shard_map(
        local, mesh=mesh, in_specs=placed, out_specs=P("tracer", "region"), check_vma=False
    )
```

```python
import functools

import jax
import jax.numpy as jnp
from jax import lax
from jax.experimental import pallas as pl
from jax.experimental.pallas import tpu as pltpu
from jax.sharding import PartitionSpec as P

MESH = pl.DeviceIdType.MESH
F32, BF16 = jnp.float32, jnp.bfloat16
LANES = 128
ROWS_DIM = (((1,), (1,)), ((), ()))


def halves(x):
    high = x.astype(BF16)
    return high, (x - high.astype(F32)).astype(BF16)


def dot(a, b):
    return jnp.dot(a, b, preferred_element_type=F32)


def dot_split(a, b):
    (a_high, a_low), (b_high, b_low) = a, halves(b)
    return dot(a_high, b_high) + (dot(a_high, b_low) + dot(a_low, b_high))


def kernel(
    cot_hbm, states_hbm, inv_hbm, wet, tiles_hbm, off, cnt, up_hbm, rel_hbm,
    out,
    tiles, inv, up, rel, adj, full_state, full_settled, gain,
    relay_out, direct_out, peer_out, merged_out,
    relay_in, direct_in, peer_in, merged_in,
    load_sem, own_sem, send_sem, recv_sem, settled_send, settled_recv, state_send, state_recv,
):
    steps, tracers_n, tr, boxes = full_state.shape
    columns, levels, _ = inv.shape
    slots = tiles.shape[0]
    ntr = tracers_n * tr
    region, tracer = lax.axis_index("region"), lax.axis_index("tracer")
    regions = lax.axis_size("region")

    sign = 2 * lax.rem(region, 2) - 1
    at = lambda distance: lax.rem(region + distance * sign + 2 * regions, regions)
    inner, outer, far, behind = at(-1), at(1), at(2), at(-2)
    others = [lax.rem(tracer + j, tracers_n) for j in range(1, tracers_n)]

    loads = [
        pltpu.make_async_copy(src, dst, load_sem.at[k])
        for k, (src, dst) in enumerate(
            [(inv_hbm, inv), (cot_hbm, adj), (up_hbm, up), (rel_hbm, rel), (tiles_hbm.at[0], tiles)]
        )
    ]
    for load in loads:
        load.start()
    own_states = [
        pltpu.make_async_copy(states_hbm.at[n], full_state.at[n, tracer], own_sem.at[n])
        for n in range(steps)
    ]
    for copy in own_states[::-1]:
        copy.start()

    barrier = pltpu.get_barrier_semaphore()
    for device in (inner, outer, behind):
        pl.semaphore_signal(barrier, inc=1, device_id={"region": device}, device_id_type=MESH)
    for other in others:
        pl.semaphore_signal(barrier, inc=1, device_id={"tracer": other}, device_id_type=MESH)
    pl.semaphore_wait(barrier, 3 + len(others))

    def state_copy(n, j):
        return pltpu.make_async_remote_copy(
            src_ref=states_hbm.at[n],
            dst_ref=full_state.at[n, tracer],
            send_sem=state_send.at[n, j],
            recv_sem=state_recv.at[n, j],
            device_id={"tracer": others[j]},
            device_id_type=MESH,
        )

    def settled_copy(i, j):
        return pltpu.make_async_remote_copy(
            src_ref=full_settled.at[i, tracer],
            dst_ref=full_settled.at[i, tracer],
            send_sem=settled_send.at[i, j],
            recv_sem=settled_recv.at[i, j],
            device_id={"tracer": others[j]},
            device_id_type=MESH,
        )

    def region_copy(i, k):
        src, dst, target = (
            (relay_out, relay_in, inner),
            (direct_out, direct_in, far),
            (peer_out, peer_in, inner),
            (merged_out, merged_in, outer),
        )[k]
        return pltpu.make_async_remote_copy(
            src_ref=src.at[i],
            dst_ref=dst.at[i],
            send_sem=send_sem.at[i, k],
            recv_sem=recv_sem.at[i, k],
            device_id={"region": target},
            device_id_type=MESH,
        )

    peers = range(len(others))
    for n in range(steps - 1, max(steps - 3, -1), -1):
        for j in peers:
            state_copy(n, j).start()

    lane = lax.broadcasted_iota(jnp.int32, (1, boxes), 1)
    wet_of = jnp.zeros((1, boxes), jnp.int32)
    for c in range(columns):
        wet_of = jnp.where(lane // levels == c, wet[c], wet_of)
    wet_mask = (lane % levels < wet_of).astype(F32)

    def tile_at(distance):
        slot, live = jnp.int32(0), jnp.int32(0)
        for k in range(slots):
            hit = jnp.logical_and(off[0, k] == distance * sign, k < cnt[0])
            slot = jnp.where(hit, k, slot)
            live = jnp.where(hit, 1, live)
        return slot, live.astype(F32)

    places = {d: tile_at(d) for d in (-2, 2, -1, 1, 0)}

    for load in loads[:4]:
        load.wait()
    per = LANES // levels
    flat = inv[...].reshape(boxes, levels)
    wide = jnp.concatenate([flat] * per, axis=1)
    row = lax.broadcasted_iota(jnp.int32, (boxes, LANES), 0)
    lanes = lax.broadcasted_iota(jnp.int32, (boxes, LANES), 1)
    wide = jnp.where((row // levels) % per == lanes // levels, wide, 0.0)
    blocks = []
    for b in range(boxes // LANES):
        span = slice(b * LANES, (b + 1) * LANES)
        high, low = halves(wide[span] * wet_mask[:, span])
        blocks.append(jnp.concatenate([high, low], axis=0))

    ident = (
        lax.broadcasted_iota(jnp.int32, (ntr, ntr), 0) == lax.broadcasted_iota(jnp.int32, (ntr, ntr), 1)
    ).astype(F32)
    own_rows = (
        lax.broadcasted_iota(jnp.int32, (tr, ntr), 0) + tracer * tr
        == lax.broadcasted_iota(jnp.int32, (tr, ntr), 1)
    ).astype(F32)
    highest = lax.Precision.HIGHEST
    uptake = halves(up[...])
    uptake_own = halves(
        lax.dot_general(own_rows, up[...], ROWS_DIM, precision=highest, preferred_element_type=F32)
    )
    release = halves(
        lax.dot_general(ident, rel[...], ROWS_DIM, precision=highest, preferred_element_type=F32)
    )

    def joined(ref, i):
        if tr % 8 == 0:
            return ref[i].reshape(ntr, boxes)
        return jnp.concatenate([ref[i, j] for j in range(tracers_n)], axis=0)

    def settle(a):
        high, low = halves(a)
        zero = jnp.zeros((tr, LANES), BF16)
        parts = []
        for b, block in enumerate(blocks):
            span = slice(b * LANES, (b + 1) * LANES)
            first = jnp.concatenate([high[:, span], high[:, span]], axis=1)
            second = jnp.concatenate([low[:, span], zero], axis=1)
            if tr % 16 == 0:
                both = dot(jnp.concatenate([first, second], axis=0), block)
                parts.append(both[:tr] + both[tr:])
            else:
                parts.append(dot(first, block) + dot(second, block))
        return jnp.concatenate(parts, axis=1)

    def make_gain(n):
        for j in peers:
            state_copy(n, j).wait_recv()
        pltpu.make_async_copy(states_hbm.at[n], full_state.at[n, tracer], own_sem.at[n]).wait()
        bent = jnp.tanh(dot_split(uptake, joined(full_state, n)))
        gain[...] = 1.0 - bent * bent

    def step(i, carry):
        n = steps - 1 - i
        settled = settle(adj[...])
        full_settled[i, tracer] = settled
        for j in peers:
            settled_copy(i, j).start()
        half = settled.astype(BF16)

        @pl.when(i == 0)
        def _():
            loads[4].wait()

        def term(distance):
            slot, live = places[distance]
            return dot(half, tiles[slot]) * live

        relay_out[i] = term(-2)
        region_copy(i, 0).start()
        direct_out[i] = term(2)
        region_copy(i, 1).start()
        near = term(1)
        region_copy(i, 0).wait_recv()
        merged_out[i] = near + relay_in[i]
        region_copy(i, 3).start()
        peer_out[i] = term(-1)
        region_copy(i, 2).start()

        @pl.when(n >= 2)
        def _():
            for j in peers:
                state_copy(n - 2, j).start()

        total = term(0)

        @pl.when(i == 0)
        def _():
            make_gain(n)

        for j in peers:
            settled_copy(i, j).wait_recv()
        weighted = gain[...] * dot_split(release, joined(full_settled, i))
        total = total + dot_split(uptake_own, weighted)

        @pl.when(n >= 1)
        def _():
            make_gain(n - 1)

        region_copy(i, 2).wait_recv()
        total = total + peer_in[i]
        region_copy(i, 1).wait_recv()
        total = total + direct_in[i]
        region_copy(i, 3).wait_recv()
        adj[...] = wet_mask * (total + merged_in[i])
        return carry

    lax.fori_loop(0, steps, step, 0)
    out[...] = adj[...]

    def drain(i, carry):
        for k in range(4):
            region_copy(i, k).wait_send()
        for j in peers:
            settled_copy(i, j).wait_send()
            state_copy(i, j).wait_send()
        return carry

    lax.fori_loop(0, steps, drain, 0)


def local(
    cotangent,
    states,
    implicit_inverse,
    wet_levels,
    explicit_tiles,
    tile_offset,
    tile_count,
    uptake_weight,
    release_weight,
):
    tr, boxes = cotangent.shape
    steps = states.shape[0]
    tracers_n = lax.axis_size("tracer")
    ntr = tracers_n * tr
    slots = explicit_tiles.shape[1]
    peers = max(tracers_n - 1, 1)
    hbm = pl.BlockSpec(memory_space=pl.ANY)
    smem = pl.BlockSpec(memory_space=pltpu.SMEM)
    message = pltpu.VMEM((steps, tr, boxes), F32)
    gathered = pltpu.VMEM((steps, tracers_n, tr, boxes), F32)
    sems = pltpu.SemaphoreType.DMA
    return pl.pallas_call(
        kernel,
        out_shape=jax.ShapeDtypeStruct((tr, boxes), F32),
        in_specs=[hbm, hbm, hbm, smem, hbm, smem, smem, hbm, hbm],
        out_specs=pl.BlockSpec(memory_space=pltpu.VMEM),
        scratch_shapes=[
            pltpu.VMEM(explicit_tiles.shape[1:], BF16),
            pltpu.VMEM(implicit_inverse.shape, F32),
            pltpu.VMEM(uptake_weight.shape, F32),
            pltpu.VMEM(release_weight.shape, F32),
            pltpu.VMEM((tr, boxes), F32),
            gathered,
            gathered,
            pltpu.VMEM((ntr, boxes), F32),
        ]
        + [message] * 8
        + [
            sems((5,)),
            sems((steps,)),
            sems((steps, 4)),
            sems((steps, 4)),
            sems((steps, peers)),
            sems((steps, peers)),
            sems((steps, peers)),
            sems((steps, peers)),
        ],
        compiler_params=pltpu.CompilerParams(
            collective_id=0, has_side_effects=True, vmem_limit_bytes=60 * 1024 * 1024
        ),
        name="adjoint_steps",
    )(
        cotangent,
        states,
        implicit_inverse,
        wet_levels,
        explicit_tiles,
        tile_offset,
        tile_count,
        uptake_weight,
        release_weight,
    )


def solution(mesh):
    placed = (
        P("tracer", "region"),
        P(None, "tracer", "region"),
        P("region", None, None),
        P("region"),
        P("region", None, None, None),
        P("region", None),
        P("region"),
        P(),
        P(),
    )
    return jax.shard_map(
        local, mesh=mesh, in_specs=placed, out_specs=P("tracer", "region"), check_vma=False
    )
```

```python
import functools

import jax
import jax.numpy as jnp
from jax import lax
from jax.experimental import pallas as pl
from jax.experimental.pallas import tpu as pltpu
from jax.sharding import PartitionSpec as P

MESH = pl.DeviceIdType.MESH
F32, BF16 = jnp.float32, jnp.bfloat16
LANES = 128
ROWS_DIM = (((1,), (1,)), ((), ()))


def halves(x):
    high = x.astype(BF16)
    return high, (x - high.astype(F32)).astype(BF16)


def dot(a, b):
    return jnp.dot(a, b, preferred_element_type=F32)


def dot_split(a, b):
    (a_high, a_low), (b_high, b_low) = a, halves(b)
    return dot(a_high, b_high) + (dot(a_high, b_low) + dot(a_low, b_high))


def kernel(
    cot_hbm, states_hbm, inv_hbm, wet, tiles_hbm, off, cnt, up_hbm, rel_hbm,
    out,
    tiles, inv, up, rel, adj, full_state, full_settled, gain,
    relay_out, direct_out, peer_out, merged_out,
    relay_in, direct_in, peer_in, merged_in,
    load_sem, own_sem, send_sem, recv_sem, settled_send, settled_recv, state_send, state_recv,
):
    steps, tracers_n, tr, boxes = full_state.shape
    columns, levels, _ = inv.shape
    slots = tiles.shape[0]
    ntr = tracers_n * tr
    region, tracer = lax.axis_index("region"), lax.axis_index("tracer")
    regions = lax.axis_size("region")

    sign = 2 * lax.rem(region, 2) - 1
    at = lambda distance: lax.rem(region + distance * sign + 2 * regions, regions)
    inner, outer, far, behind = at(-1), at(1), at(2), at(-2)
    others = [lax.rem(tracer + j, tracers_n) for j in range(1, tracers_n)]

    barrier = pltpu.get_barrier_semaphore()
    for device in (inner, outer, far, behind):
        pl.semaphore_signal(barrier, inc=1, device_id={"region": device}, device_id_type=MESH)
    for other in others:
        pl.semaphore_signal(barrier, inc=1, device_id={"tracer": other}, device_id_type=MESH)

    loads = [
        pltpu.make_async_copy(src, dst, load_sem.at[k])
        for k, (src, dst) in enumerate(
            [(inv_hbm, inv), (cot_hbm, adj), (up_hbm, up), (rel_hbm, rel), (tiles_hbm.at[0], tiles)]
        )
    ]
    for load in loads:
        load.start()
    own_states = [
        pltpu.make_async_copy(states_hbm.at[n], full_state.at[n, tracer], own_sem.at[n])
        for n in range(steps)
    ]
    for copy in own_states[::-1]:
        copy.start()

    def state_copy(n, j):
        return pltpu.make_async_remote_copy(
            src_ref=states_hbm.at[n],
            dst_ref=full_state.at[n, tracer],
            send_sem=state_send.at[n, j],
            recv_sem=state_recv.at[n, j],
            device_id={"tracer": others[j]},
            device_id_type=MESH,
        )

    def settled_copy(i, j):
        return pltpu.make_async_remote_copy(
            src_ref=full_settled.at[i, tracer],
            dst_ref=full_settled.at[i, tracer],
            send_sem=settled_send.at[i, j],
            recv_sem=settled_recv.at[i, j],
            device_id={"tracer": others[j]},
            device_id_type=MESH,
        )

    def region_copy(i, k):
        src, dst, target = (
            (relay_out, relay_in, behind),
            (direct_out, direct_in, far),
            (peer_out, peer_in, inner),
            (merged_out, merged_in, outer),
        )[k]
        return pltpu.make_async_remote_copy(
            src_ref=src.at[i],
            dst_ref=dst.at[i],
            send_sem=send_sem.at[i, k],
            recv_sem=recv_sem.at[i, k],
            device_id={"region": target},
            device_id_type=MESH,
        )

    peers = range(len(others))

    lane = lax.broadcasted_iota(jnp.int32, (1, boxes), 1)
    wet_of = jnp.zeros((1, boxes), jnp.int32)
    for c in range(columns):
        wet_of = jnp.where(lane // levels == c, wet[c], wet_of)
    wet_mask = (lane % levels < wet_of).astype(F32)

    def tile_at(distance):
        slot, live = jnp.int32(0), jnp.int32(0)
        for k in range(slots):
            hit = jnp.logical_and(off[0, k] == distance * sign, k < cnt[0])
            slot = jnp.where(hit, k, slot)
            live = jnp.where(hit, 1, live)
        return slot, live.astype(F32)

    places = {d: tile_at(d) for d in (-2, 2, -1, 1, 0)}

    for load in loads[:4]:
        load.wait()
    per = LANES // levels
    flat = inv[...].reshape(boxes, levels)
    wide = jnp.concatenate([flat] * per, axis=1)
    row = lax.broadcasted_iota(jnp.int32, (boxes, LANES), 0)
    lanes = lax.broadcasted_iota(jnp.int32, (boxes, LANES), 1)
    wide = jnp.where((row // levels) % per == lanes // levels, wide, 0.0)
    blocks = []
    for b in range(boxes // LANES):
        span = slice(b * LANES, (b + 1) * LANES)
        high, low = halves(wide[span] * wet_mask[:, span])
        blocks.append(jnp.concatenate([high, low], axis=0))

    ident = (
        lax.broadcasted_iota(jnp.int32, (ntr, ntr), 0) == lax.broadcasted_iota(jnp.int32, (ntr, ntr), 1)
    ).astype(F32)
    own_rows = (
        lax.broadcasted_iota(jnp.int32, (tr, ntr), 0) + tracer * tr
        == lax.broadcasted_iota(jnp.int32, (tr, ntr), 1)
    ).astype(F32)
    highest = lax.Precision.HIGHEST
    uptake = halves(up[...])
    uptake_own = halves(
        lax.dot_general(own_rows, up[...], ROWS_DIM, precision=highest, preferred_element_type=F32)
    )
    release = halves(
        lax.dot_general(ident, rel[...], ROWS_DIM, precision=highest, preferred_element_type=F32)
    )

    def joined(ref, i):
        if tr % 8 == 0:
            return ref[i].reshape(ntr, boxes)
        return jnp.concatenate([ref[i, j] for j in range(tracers_n)], axis=0)

    def settle(a):
        high, low = halves(a)
        zero = jnp.zeros((tr, LANES), BF16)
        parts = []
        for b, block in enumerate(blocks):
            span = slice(b * LANES, (b + 1) * LANES)
            first = jnp.concatenate([high[:, span], high[:, span]], axis=1)
            second = jnp.concatenate([low[:, span], zero], axis=1)
            if tr % 16 == 0:
                both = dot(jnp.concatenate([first, second], axis=0), block)
                parts.append(both[:tr] + both[tr:])
            else:
                parts.append(dot(first, block) + dot(second, block))
        return jnp.concatenate(parts, axis=1)

    def make_gain(n):
        for j in peers:
            state_copy(n, j).wait_recv()
        pltpu.make_async_copy(states_hbm.at[n], full_state.at[n, tracer], own_sem.at[n]).wait()
        bent = jnp.tanh(dot_split(uptake, joined(full_state, n)))
        gain[...] = 1.0 - bent * bent

    def step(i, first):
        n = steps - 1 - i
        settled = settle(adj[...])
        full_settled[i, tracer] = settled
        half = settled.astype(BF16)

        def term(distance):
            slot, live = places[distance]
            return dot(half, tiles[slot]) * live

        def send_settled():
            for j in peers:
                settled_copy(i, j).start()

        if first:
            loads[4].wait()
            relay_out[i] = term(-2)
            direct_out[i] = term(2)
            peer_out[i] = term(-1)
            merged_out[i] = term(1)
            total = term(0)
            pl.semaphore_wait(barrier, 4 + len(others))
            region_copy(i, 0).start()
            region_copy(i, 1).start()
            region_copy(i, 3).start()
            for j in peers:
                state_copy(n, j).start()
            send_settled()
            region_copy(i, 2).start()
            if steps > 1:
                for j in peers:
                    state_copy(n - 1, j).start()
        else:
            send_settled()
            relay_out[i] = term(-2)
            region_copy(i, 0).start()
            direct_out[i] = term(2)
            region_copy(i, 1).start()
            merged_out[i] = term(1)
            region_copy(i, 3).start()
            peer_out[i] = term(-1)
            region_copy(i, 2).start()
            total = term(0)

        @pl.when(n >= 2)
        def _():
            for j in peers:
                state_copy(n - 2, j).start()

        if first:
            make_gain(n)
        for j in peers:
            settled_copy(i, j).wait_recv()
        weighted = gain[...] * dot_split(release, joined(full_settled, i))
        total = total + dot_split(uptake_own, weighted)

        @pl.when(n >= 1)
        def _():
            make_gain(n - 1)

        region_copy(i, 2).wait_recv()
        total = total + peer_in[i]
        region_copy(i, 1).wait_recv()
        total = total + direct_in[i]
        region_copy(i, 3).wait_recv()
        total = total + merged_in[i]
        region_copy(i, 0).wait_recv()
        adj[...] = wet_mask * (total + relay_in[i])

    def later_step(i, carry):
        step(i, False)
        return carry

    step(0, True)
    lax.fori_loop(1, steps, later_step, 0)
    out[...] = adj[...]

    def drain(i, carry):
        for k in range(4):
            region_copy(i, k).wait_send()
        for j in peers:
            settled_copy(i, j).wait_send()
            state_copy(i, j).wait_send()
        return carry

    lax.fori_loop(0, steps, drain, 0)


def local(
    cotangent,
    states,
    implicit_inverse,
    wet_levels,
    explicit_tiles,
    tile_offset,
    tile_count,
    uptake_weight,
    release_weight,
):
    tr, boxes = cotangent.shape
    steps = states.shape[0]
    tracers_n = lax.axis_size("tracer")
    ntr = tracers_n * tr
    slots = explicit_tiles.shape[1]
    peers = max(tracers_n - 1, 1)
    hbm = pl.BlockSpec(memory_space=pl.ANY)
    smem = pl.BlockSpec(memory_space=pltpu.SMEM)
    message = pltpu.VMEM((steps, tr, boxes), F32)
    gathered = pltpu.VMEM((steps, tracers_n, tr, boxes), F32)
    sems = pltpu.SemaphoreType.DMA
    return pl.pallas_call(
        kernel,
        out_shape=jax.ShapeDtypeStruct((tr, boxes), F32),
        in_specs=[hbm, hbm, hbm, smem, hbm, smem, smem, hbm, hbm],
        out_specs=pl.BlockSpec(memory_space=pltpu.VMEM),
        scratch_shapes=[
            pltpu.VMEM(explicit_tiles.shape[1:], BF16),
            pltpu.VMEM(implicit_inverse.shape, F32),
            pltpu.VMEM(uptake_weight.shape, F32),
            pltpu.VMEM(release_weight.shape, F32),
            pltpu.VMEM((tr, boxes), F32),
            gathered,
            gathered,
            pltpu.VMEM((ntr, boxes), F32),
        ]
        + [message] * 8
        + [
            sems((5,)),
            sems((steps,)),
            sems((steps, 4)),
            sems((steps, 4)),
            sems((steps, peers)),
            sems((steps, peers)),
            sems((steps, peers)),
            sems((steps, peers)),
        ],
        compiler_params=pltpu.CompilerParams(
            collective_id=0, has_side_effects=True, vmem_limit_bytes=60 * 1024 * 1024
        ),
        name="adjoint_steps",
    )(
        cotangent,
        states,
        implicit_inverse,
        wet_levels,
        explicit_tiles,
        tile_offset,
        tile_count,
        uptake_weight,
        release_weight,
    )


def solution(mesh):
    placed = (
        P("tracer", "region"),
        P(None, "tracer", "region"),
        P("region", None, None),
        P("region"),
        P("region", None, None, None),
        P("region", None),
        P("region"),
        P(),
        P(),
    )
    return jax.shard_map(
        local, mesh=mesh, in_specs=placed, out_specs=P("tracer", "region"), check_vma=False
    )
```

```python
import functools

import jax
import jax.numpy as jnp
from jax import lax
from jax.experimental import pallas as pl
from jax.experimental.pallas import tpu as pltpu
from jax.sharding import PartitionSpec as P

MESH = pl.DeviceIdType.MESH
F32, BF16 = jnp.float32, jnp.bfloat16
LANES = 128
ROWS_DIM = (((1,), (1,)), ((), ()))


def halves(x):
    high = x.astype(BF16)
    return high, (x - high.astype(F32)).astype(BF16)


def dot(a, b):
    return jnp.dot(a, b, preferred_element_type=F32)


def dot_split(a, b):
    (a_high, a_low), (b_high, b_low) = a, halves(b)
    return dot(a_high, b_high) + (dot(a_high, b_low) + dot(a_low, b_high))


def kernel(
    cot_hbm, states_hbm, inv_hbm, wet, tiles_hbm, off, cnt, up_hbm, rel_hbm,
    out,
    tiles, inv, up, rel, adj, full_state, full_settled, gain,
    relay_out, direct_out, peer_out, merged_out,
    relay_in, direct_in, peer_in, merged_in,
    load_sem, own_sem, send_sem, recv_sem, settled_send, settled_recv, state_send, state_recv,
):
    steps, tracers_n, tr, boxes = full_state.shape
    columns, levels, _ = inv.shape
    slots = tiles.shape[0]
    ntr = tracers_n * tr
    region, tracer = lax.axis_index("region"), lax.axis_index("tracer")
    regions = lax.axis_size("region")

    sign = 2 * lax.rem(region, 2) - 1
    at = lambda distance: lax.rem(region + distance * sign + 2 * regions, regions)
    inner, outer, far, behind = at(-1), at(1), at(2), at(-2)
    others = [lax.rem(tracer + j, tracers_n) for j in range(1, tracers_n)]

    barrier = pltpu.get_barrier_semaphore()
    for device in (inner, outer, far, behind):
        pl.semaphore_signal(barrier, inc=1, device_id={"region": device}, device_id_type=MESH)
    for other in others:
        pl.semaphore_signal(barrier, inc=1, device_id={"tracer": other}, device_id_type=MESH)

    loads = [
        pltpu.make_async_copy(src, dst, load_sem.at[k])
        for k, (src, dst) in enumerate(
            [(inv_hbm, inv), (cot_hbm, adj), (up_hbm, up), (rel_hbm, rel), (tiles_hbm.at[0], tiles)]
        )
    ]
    for load in loads:
        load.start()
    own_states = [
        pltpu.make_async_copy(states_hbm.at[n], full_state.at[n, tracer], own_sem.at[n])
        for n in range(steps)
    ]
    for copy in own_states[::-1]:
        copy.start()

    def state_copy(n, j):
        return pltpu.make_async_remote_copy(
            src_ref=states_hbm.at[n],
            dst_ref=full_state.at[n, tracer],
            send_sem=state_send.at[n, j],
            recv_sem=state_recv.at[n, j],
            device_id={"tracer": others[j]},
            device_id_type=MESH,
        )

    def settled_copy(i, j):
        return pltpu.make_async_remote_copy(
            src_ref=full_settled.at[i, tracer],
            dst_ref=full_settled.at[i, tracer],
            send_sem=settled_send.at[i, j],
            recv_sem=settled_recv.at[i, j],
            device_id={"tracer": others[j]},
            device_id_type=MESH,
        )

    def region_copy(i, k):
        src, dst, target = (
            (relay_out, relay_in, behind),
            (direct_out, direct_in, far),
            (peer_out, peer_in, inner),
            (merged_out, merged_in, outer),
        )[k]
        return pltpu.make_async_remote_copy(
            src_ref=src.at[i],
            dst_ref=dst.at[i],
            send_sem=send_sem.at[i, k],
            recv_sem=recv_sem.at[i, k],
            device_id={"region": target},
            device_id_type=MESH,
        )

    peers = range(len(others))

    lane = lax.broadcasted_iota(jnp.int32, (1, boxes), 1)
    wet_of = jnp.zeros((1, boxes), jnp.int32)
    for c in range(columns):
        wet_of = jnp.where(lane // levels == c, wet[c], wet_of)
    wet_mask = (lane % levels < wet_of).astype(F32)

    def tile_at(distance):
        slot, live = jnp.int32(0), jnp.int32(0)
        for k in range(slots):
            hit = jnp.logical_and(off[0, k] == distance * sign, k < cnt[0])
            slot = jnp.where(hit, k, slot)
            live = jnp.where(hit, 1, live)
        return slot, live.astype(F32)

    places = {d: tile_at(d) for d in (-2, 2, -1, 1, 0)}

    for load in loads[:4]:
        load.wait()
    per = LANES // levels
    flat = inv[...].reshape(boxes, levels)
    wide = jnp.concatenate([flat] * per, axis=1)
    row = lax.broadcasted_iota(jnp.int32, (boxes, LANES), 0)
    lanes = lax.broadcasted_iota(jnp.int32, (boxes, LANES), 1)
    wide = jnp.where((row // levels) % per == lanes // levels, wide, 0.0)
    blocks = []
    for b in range(boxes // LANES):
        span = slice(b * LANES, (b + 1) * LANES)
        high, low = halves(wide[span] * wet_mask[:, span])
        blocks.append(jnp.concatenate([high, low], axis=0))

    ident = (
        lax.broadcasted_iota(jnp.int32, (ntr, ntr), 0) == lax.broadcasted_iota(jnp.int32, (ntr, ntr), 1)
    ).astype(F32)
    own_rows = (
        lax.broadcasted_iota(jnp.int32, (tr, ntr), 0) + tracer * tr
        == lax.broadcasted_iota(jnp.int32, (tr, ntr), 1)
    ).astype(F32)
    highest = lax.Precision.HIGHEST
    uptake = halves(up[...])
    uptake_own = halves(
        lax.dot_general(own_rows, up[...], ROWS_DIM, precision=highest, preferred_element_type=F32)
    )
    release = halves(
        lax.dot_general(ident, rel[...], ROWS_DIM, precision=highest, preferred_element_type=F32)
    )

    def joined(ref, i):
        if tr % 8 == 0:
            return ref[i].reshape(ntr, boxes)
        return jnp.concatenate([ref[i, j] for j in range(tracers_n)], axis=0)

    def settle(a):
        high, low = halves(a)
        zero = jnp.zeros((tr, LANES), BF16)
        parts = []
        for b, block in enumerate(blocks):
            span = slice(b * LANES, (b + 1) * LANES)
            first = jnp.concatenate([high[:, span], high[:, span]], axis=1)
            second = jnp.concatenate([low[:, span], zero], axis=1)
            if tr % 16 == 0:
                both = dot(jnp.concatenate([first, second], axis=0), block)
                parts.append(both[:tr] + both[tr:])
            else:
                parts.append(dot(first, block) + dot(second, block))
        return jnp.concatenate(parts, axis=1)

    def make_gain(n):
        for j in peers:
            state_copy(n, j).wait_recv()
        pltpu.make_async_copy(states_hbm.at[n], full_state.at[n, tracer], own_sem.at[n]).wait()
        bent = jnp.tanh(dot_split(uptake, joined(full_state, n)))
        gain[...] = 1.0 - bent * bent

    def step(i, first):
        n = steps - 1 - i
        settled = settle(adj[...])
        full_settled[i, tracer] = settled
        half = settled.astype(BF16)

        def term(distance):
            slot, live = places[distance]
            return dot(half, tiles[slot]) * live

        def send_settled():
            for j in peers:
                settled_copy(i, j).start()

        if first:
            loads[4].wait()
            relay_out[i] = term(-2)
            direct_out[i] = term(2)
            peer_out[i] = term(-1)
            merged_out[i] = term(1)
            total = term(0)
            pl.semaphore_wait(barrier, 4 + len(others))
            region_copy(i, 0).start()
            region_copy(i, 1).start()
            region_copy(i, 3).start()
            for j in peers:
                state_copy(n, j).start()
            send_settled()
            region_copy(i, 2).start()
            if steps > 1:
                for j in peers:
                    state_copy(n - 1, j).start()
        else:
            send_settled()
            direct_out[i] = term(2)
            region_copy(i, 1).start()
            relay_out[i] = term(-2)
            region_copy(i, 0).start()
            merged_out[i] = term(1)
            region_copy(i, 3).start()
            peer_out[i] = term(-1)
            region_copy(i, 2).start()
            total = term(0)

        @pl.when(n >= 2)
        def _():
            for j in peers:
                state_copy(n - 2, j).start()

        make_gain(n)
        for j in peers:
            settled_copy(i, j).wait_recv()
        weighted = gain[...] * dot_split(release, joined(full_settled, i))
        total = total + dot_split(uptake_own, weighted)

        region_copy(i, 2).wait_recv()
        total = total + peer_in[i]
        region_copy(i, 1).wait_recv()
        total = total + direct_in[i]
        region_copy(i, 3).wait_recv()
        total = total + merged_in[i]
        region_copy(i, 0).wait_recv()
        adj[...] = wet_mask * (total + relay_in[i])

    def later_step(i, carry):
        step(i, False)
        return carry

    step(0, True)
    lax.fori_loop(1, steps, later_step, 0)
    out[...] = adj[...]

    def drain(i, carry):
        for k in range(4):
            region_copy(i, k).wait_send()
        for j in peers:
            settled_copy(i, j).wait_send()
            state_copy(i, j).wait_send()
        return carry

    lax.fori_loop(0, steps, drain, 0)


def local(
    cotangent,
    states,
    implicit_inverse,
    wet_levels,
    explicit_tiles,
    tile_offset,
    tile_count,
    uptake_weight,
    release_weight,
):
    tr, boxes = cotangent.shape
    steps = states.shape[0]
    tracers_n = lax.axis_size("tracer")
    ntr = tracers_n * tr
    slots = explicit_tiles.shape[1]
    peers = max(tracers_n - 1, 1)
    hbm = pl.BlockSpec(memory_space=pl.ANY)
    smem = pl.BlockSpec(memory_space=pltpu.SMEM)
    message = pltpu.VMEM((steps, tr, boxes), F32)
    gathered = pltpu.VMEM((steps, tracers_n, tr, boxes), F32)
    sems = pltpu.SemaphoreType.DMA
    return pl.pallas_call(
        kernel,
        out_shape=jax.ShapeDtypeStruct((tr, boxes), F32),
        in_specs=[hbm, hbm, hbm, smem, hbm, smem, smem, hbm, hbm],
        out_specs=pl.BlockSpec(memory_space=pltpu.VMEM),
        scratch_shapes=[
            pltpu.VMEM(explicit_tiles.shape[1:], BF16),
            pltpu.VMEM(implicit_inverse.shape, F32),
            pltpu.VMEM(uptake_weight.shape, F32),
            pltpu.VMEM(release_weight.shape, F32),
            pltpu.VMEM((tr, boxes), F32),
            gathered,
            gathered,
            pltpu.VMEM((ntr, boxes), F32),
        ]
        + [message] * 8
        + [
            sems((5,)),
            sems((steps,)),
            sems((steps, 4)),
            sems((steps, 4)),
            sems((steps, peers)),
            sems((steps, peers)),
            sems((steps, peers)),
            sems((steps, peers)),
        ],
        compiler_params=pltpu.CompilerParams(
            collective_id=0, has_side_effects=True, vmem_limit_bytes=60 * 1024 * 1024
        ),
        name="adjoint_steps",
    )(
        cotangent,
        states,
        implicit_inverse,
        wet_levels,
        explicit_tiles,
        tile_offset,
        tile_count,
        uptake_weight,
        release_weight,
    )


def solution(mesh):
    placed = (
        P("tracer", "region"),
        P(None, "tracer", "region"),
        P("region", None, None),
        P("region"),
        P("region", None, None, None),
        P("region", None),
        P("region"),
        P(),
        P(),
    )
    return jax.shard_map(
        local, mesh=mesh, in_specs=placed, out_specs=P("tracer", "region"), check_vma=False
    )
```

```python
import functools

import jax
import jax.numpy as jnp
from jax import lax
from jax.experimental import pallas as pl
from jax.experimental.pallas import tpu as pltpu
from jax.sharding import PartitionSpec as P

MESH = pl.DeviceIdType.MESH
F32, BF16 = jnp.float32, jnp.bfloat16
LANES = 128
ROWS_DIM = (((1,), (1,)), ((), ()))


def halves(x):
    high = x.astype(BF16)
    return high, (x - high.astype(F32)).astype(BF16)


def dot(a, b):
    return jnp.dot(a, b, preferred_element_type=F32)


def dot_split(a, b):
    (a_high, a_low), (b_high, b_low) = a, halves(b)
    return dot(a_high, b_high) + (dot(a_high, b_low) + dot(a_low, b_high))


def kernel(
    cot_hbm, states_hbm, inv_hbm, wet, tiles_hbm, off, cnt, up_hbm, rel_hbm,
    out,
    tiles, inv, up, rel, adj, full_state, full_settled, gain,
    relay_out, direct_out, peer_out, merged_out,
    relay_in, direct_in, peer_in, merged_in,
    load_sem, own_sem, send_sem, recv_sem, settled_send, settled_recv, state_send, state_recv,
):
    steps, tracers_n, tr, boxes = full_state.shape
    columns, levels, _ = inv.shape
    slots = tiles.shape[0]
    ntr = tracers_n * tr
    region, tracer = lax.axis_index("region"), lax.axis_index("tracer")
    regions = lax.axis_size("region")

    sign = 2 * lax.rem(region, 2) - 1
    at = lambda distance: lax.rem(region + distance * sign + 2 * regions, regions)
    inner, outer, far, behind = at(-1), at(1), at(2), at(-2)
    others = [lax.rem(tracer + j, tracers_n) for j in range(1, tracers_n)]

    barrier = pltpu.get_barrier_semaphore()
    for device in (inner, outer, far, behind):
        pl.semaphore_signal(barrier, inc=1, device_id={"region": device}, device_id_type=MESH)
    for other in others:
        pl.semaphore_signal(barrier, inc=1, device_id={"tracer": other}, device_id_type=MESH)

    loads = [
        pltpu.make_async_copy(src, dst, load_sem.at[k])
        for k, (src, dst) in enumerate(
            [(inv_hbm, inv), (cot_hbm, adj), (up_hbm, up), (rel_hbm, rel), (tiles_hbm.at[0], tiles)]
        )
    ]
    for load in loads:
        load.start()
    own_states = [
        pltpu.make_async_copy(states_hbm.at[n], full_state.at[n, tracer], own_sem.at[n])
        for n in range(steps)
    ]
    for copy in own_states[::-1]:
        copy.start()

    def state_copy(n, j):
        return pltpu.make_async_remote_copy(
            src_ref=states_hbm.at[n],
            dst_ref=full_state.at[n, tracer],
            send_sem=state_send.at[n, j],
            recv_sem=state_recv.at[n, j],
            device_id={"tracer": others[j]},
            device_id_type=MESH,
        )

    def settled_copy(i, j):
        return pltpu.make_async_remote_copy(
            src_ref=full_settled.at[i, tracer],
            dst_ref=full_settled.at[i, tracer],
            send_sem=settled_send.at[i, j],
            recv_sem=settled_recv.at[i, j],
            device_id={"tracer": others[j]},
            device_id_type=MESH,
        )

    def region_copy(i, k):
        src, dst, target = (
            (relay_out, relay_in, behind),
            (direct_out, direct_in, far),
            (peer_out, peer_in, inner),
            (merged_out, merged_in, outer),
        )[k]
        return pltpu.make_async_remote_copy(
            src_ref=src.at[i],
            dst_ref=dst.at[i],
            send_sem=send_sem.at[i, k],
            recv_sem=recv_sem.at[i, k],
            device_id={"region": target},
            device_id_type=MESH,
        )

    peers = range(len(others))

    lane = lax.broadcasted_iota(jnp.int32, (1, boxes), 1)
    wet_of = jnp.zeros((1, boxes), jnp.int32)
    for c in range(columns):
        wet_of = jnp.where(lane // levels == c, wet[c], wet_of)
    wet_mask = (lane % levels < wet_of).astype(F32)

    def tile_at(distance):
        slot, live = jnp.int32(0), jnp.int32(0)
        for k in range(slots):
            hit = jnp.logical_and(off[0, k] == distance * sign, k < cnt[0])
            slot = jnp.where(hit, k, slot)
            live = jnp.where(hit, 1, live)
        return slot, live.astype(F32)

    places = {d: tile_at(d) for d in (-2, 2, -1, 1, 0)}

    for load in loads[:4]:
        load.wait()
    per = LANES // levels
    flat = inv[...].reshape(boxes, levels)
    wide = jnp.concatenate([flat] * per, axis=1)
    row = lax.broadcasted_iota(jnp.int32, (boxes, LANES), 0)
    lanes = lax.broadcasted_iota(jnp.int32, (boxes, LANES), 1)
    wide = jnp.where((row // levels) % per == lanes // levels, wide, 0.0)
    blocks = []
    for b in range(boxes // LANES):
        span = slice(b * LANES, (b + 1) * LANES)
        high, low = halves(wide[span] * wet_mask[:, span])
        blocks.append(jnp.concatenate([high, low], axis=0))

    ident = (
        lax.broadcasted_iota(jnp.int32, (ntr, ntr), 0) == lax.broadcasted_iota(jnp.int32, (ntr, ntr), 1)
    ).astype(F32)
    own_rows = (
        lax.broadcasted_iota(jnp.int32, (tr, ntr), 0) + tracer * tr
        == lax.broadcasted_iota(jnp.int32, (tr, ntr), 1)
    ).astype(F32)
    highest = lax.Precision.HIGHEST
    uptake = halves(up[...])
    uptake_own = halves(
        lax.dot_general(own_rows, up[...], ROWS_DIM, precision=highest, preferred_element_type=F32)
    )
    release = halves(
        lax.dot_general(ident, rel[...], ROWS_DIM, precision=highest, preferred_element_type=F32)
    )

    def joined(ref, i):
        if tr % 8 == 0:
            return ref[i].reshape(ntr, boxes)
        return jnp.concatenate([ref[i, j] for j in range(tracers_n)], axis=0)

    def settle(a):
        high, low = halves(a)
        zero = jnp.zeros((tr, LANES), BF16)
        parts = []
        for b, block in enumerate(blocks):
            span = slice(b * LANES, (b + 1) * LANES)
            first = jnp.concatenate([high[:, span], high[:, span]], axis=1)
            second = jnp.concatenate([low[:, span], zero], axis=1)
            if tr % 16 == 0:
                both = dot(jnp.concatenate([first, second], axis=0), block)
                parts.append(both[:tr] + both[tr:])
            else:
                parts.append(dot(first, block) + dot(second, block))
        return jnp.concatenate(parts, axis=1)

    def make_gain(n):
        for j in peers:
            state_copy(n, j).wait_recv()
        pltpu.make_async_copy(states_hbm.at[n], full_state.at[n, tracer], own_sem.at[n]).wait()
        bent = jnp.tanh(dot_split(uptake, joined(full_state, n)))
        gain[...] = 1.0 - bent * bent

    def drain(i):
        for k in range(4):
            region_copy(i, k).wait_send()
        for j in peers:
            settled_copy(i, j).wait_send()
            state_copy(steps - 1 - i, j).wait_send()

    def step(i, first):
        n = steps - 1 - i
        settled = settle(adj[...])
        full_settled[i, tracer] = settled
        half = settled.astype(BF16)

        def term(distance):
            slot, live = places[distance]
            return dot(half, tiles[slot]) * live

        def send_settled():
            for j in peers:
                settled_copy(i, j).start()

        if first:
            loads[4].wait()
            relay_out[i] = term(-2)
            direct_out[i] = term(2)
            peer_out[i] = term(-1)
            merged_out[i] = term(1)
            total = term(0)
            pl.semaphore_wait(barrier, 4 + len(others))
            region_copy(i, 0).start()
            region_copy(i, 1).start()
            region_copy(i, 3).start()
            for j in peers:
                state_copy(n, j).start()
            send_settled()
            region_copy(i, 2).start()
            if steps > 1:
                for j in peers:
                    state_copy(n - 1, j).start()
        else:
            direct_out[i] = term(2)
            region_copy(i, 1).start()
            send_settled()
            relay_out[i] = term(-2)
            region_copy(i, 0).start()
            merged_out[i] = term(1)
            region_copy(i, 3).start()
            peer_out[i] = term(-1)
            region_copy(i, 2).start()
            total = term(0)

        @pl.when(n >= 2)
        def _():
            for j in peers:
                state_copy(n - 2, j).start()

        if not first:
            drain(i - 1)
        make_gain(n)
        for j in peers:
            settled_copy(i, j).wait_recv()
        weighted = gain[...] * dot_split(release, joined(full_settled, i))
        total = total + dot_split(uptake_own, weighted)

        region_copy(i, 2).wait_recv()
        total = total + peer_in[i]
        region_copy(i, 1).wait_recv()
        total = total + direct_in[i]
        region_copy(i, 3).wait_recv()
        total = total + merged_in[i]
        region_copy(i, 0).wait_recv()
        adj[...] = wet_mask * (total + relay_in[i])

    def later_step(i, carry):
        step(i, False)
        return carry

    step(0, True)
    lax.fori_loop(1, steps, later_step, 0)
    out[...] = adj[...]
    drain(steps - 1)


def local(
    cotangent,
    states,
    implicit_inverse,
    wet_levels,
    explicit_tiles,
    tile_offset,
    tile_count,
    uptake_weight,
    release_weight,
):
    tr, boxes = cotangent.shape
    steps = states.shape[0]
    tracers_n = lax.axis_size("tracer")
    ntr = tracers_n * tr
    slots = explicit_tiles.shape[1]
    peers = max(tracers_n - 1, 1)
    hbm = pl.BlockSpec(memory_space=pl.ANY)
    smem = pl.BlockSpec(memory_space=pltpu.SMEM)
    message = pltpu.VMEM((steps, tr, boxes), F32)
    gathered = pltpu.VMEM((steps, tracers_n, tr, boxes), F32)
    sems = pltpu.SemaphoreType.DMA
    return pl.pallas_call(
        kernel,
        out_shape=jax.ShapeDtypeStruct((tr, boxes), F32),
        in_specs=[hbm, hbm, hbm, smem, hbm, smem, smem, hbm, hbm],
        out_specs=pl.BlockSpec(memory_space=pltpu.VMEM),
        scratch_shapes=[
            pltpu.VMEM(explicit_tiles.shape[1:], BF16),
            pltpu.VMEM(implicit_inverse.shape, F32),
            pltpu.VMEM(uptake_weight.shape, F32),
            pltpu.VMEM(release_weight.shape, F32),
            pltpu.VMEM((tr, boxes), F32),
            gathered,
            gathered,
            pltpu.VMEM((ntr, boxes), F32),
        ]
        + [message] * 8
        + [
            sems((5,)),
            sems((steps,)),
            sems((steps, 4)),
            sems((steps, 4)),
            sems((steps, peers)),
            sems((steps, peers)),
            sems((steps, peers)),
            sems((steps, peers)),
        ],
        compiler_params=pltpu.CompilerParams(
            collective_id=0, has_side_effects=True, vmem_limit_bytes=60 * 1024 * 1024
        ),
        name="adjoint_steps",
    )(
        cotangent,
        states,
        implicit_inverse,
        wet_levels,
        explicit_tiles,
        tile_offset,
        tile_count,
        uptake_weight,
        release_weight,
    )


def solution(mesh):
    placed = (
        P("tracer", "region"),
        P(None, "tracer", "region"),
        P("region", None, None),
        P("region"),
        P("region", None, None, None),
        P("region", None),
        P("region"),
        P(),
        P(),
    )
    return jax.shard_map(
        local, mesh=mesh, in_specs=placed, out_specs=P("tracer", "region"), check_vma=False
    )
```

```python
import functools

import jax
import jax.numpy as jnp
from jax import lax
from jax.experimental import pallas as pl
from jax.experimental.pallas import tpu as pltpu
from jax.sharding import PartitionSpec as P

MESH = pl.DeviceIdType.MESH
F32, BF16 = jnp.float32, jnp.bfloat16
LANES = 128
ROWS_DIM = (((1,), (1,)), ((), ()))


def halves(x):
    high = x.astype(BF16)
    return high, (x - high.astype(F32)).astype(BF16)


def dot(a, b):
    return jnp.dot(a, b, preferred_element_type=F32)


def dot_split(a, b):
    (a_high, a_low), (b_high, b_low) = a, halves(b)
    return dot(
        jnp.concatenate([a_high, a_high, a_low], axis=1),
        jnp.concatenate([b_high, b_low, b_high], axis=0),
    )


def kernel(
    cot_hbm, states_hbm, inv_hbm, wet, tiles_hbm, off, cnt, up_hbm, rel_hbm,
    out,
    tiles, inv, up, rel, adj, full_state, full_settled, gain,
    relay_out, direct_out, peer_out, merged_out,
    relay_in, direct_in, peer_in, merged_in,
    load_sem, own_sem, send_sem, recv_sem, settled_send, settled_recv, state_send, state_recv,
):
    steps, tracers_n, tr, boxes = full_state.shape
    columns, levels, _ = inv.shape
    slots = tiles.shape[0]
    ntr = tracers_n * tr
    region, tracer = lax.axis_index("region"), lax.axis_index("tracer")
    regions = lax.axis_size("region")

    sign = 2 * lax.rem(region, 2) - 1
    at = lambda distance: lax.rem(region + distance * sign + 2 * regions, regions)
    inner, outer, far, behind = at(-1), at(1), at(2), at(-2)
    others = [lax.rem(tracer + j, tracers_n) for j in range(1, tracers_n)]

    barrier = pltpu.get_barrier_semaphore()
    for device in (inner, outer, far, behind):
        pl.semaphore_signal(barrier, inc=1, device_id={"region": device}, device_id_type=MESH)
    for other in others:
        pl.semaphore_signal(barrier, inc=1, device_id={"tracer": other}, device_id_type=MESH)

    loads = [
        pltpu.make_async_copy(src, dst, load_sem.at[k])
        for k, (src, dst) in enumerate(
            [(inv_hbm, inv), (cot_hbm, adj), (up_hbm, up), (rel_hbm, rel), (tiles_hbm.at[0], tiles)]
        )
    ]
    for load in loads:
        load.start()
    own_states = [
        pltpu.make_async_copy(states_hbm.at[n], full_state.at[n, tracer], own_sem.at[n])
        for n in range(steps)
    ]
    for copy in own_states[::-1]:
        copy.start()

    def state_copy(n, j):
        return pltpu.make_async_remote_copy(
            src_ref=states_hbm.at[n],
            dst_ref=full_state.at[n, tracer],
            send_sem=state_send.at[n, j],
            recv_sem=state_recv.at[n, j],
            device_id={"tracer": others[j]},
            device_id_type=MESH,
        )

    def settled_copy(i, j):
        return pltpu.make_async_remote_copy(
            src_ref=full_settled.at[i, tracer],
            dst_ref=full_settled.at[i, tracer],
            send_sem=settled_send.at[i, j],
            recv_sem=settled_recv.at[i, j],
            device_id={"tracer": others[j]},
            device_id_type=MESH,
        )

    def region_copy(i, k):
        src, dst, target = (
            (relay_out, relay_in, behind),
            (direct_out, direct_in, far),
            (peer_out, peer_in, inner),
            (merged_out, merged_in, outer),
        )[k]
        return pltpu.make_async_remote_copy(
            src_ref=src.at[i],
            dst_ref=dst.at[i],
            send_sem=send_sem.at[i, k],
            recv_sem=recv_sem.at[i, k],
            device_id={"region": target},
            device_id_type=MESH,
        )

    peers = range(len(others))

    lane = lax.broadcasted_iota(jnp.int32, (1, boxes), 1)
    wet_of = jnp.zeros((1, boxes), jnp.int32)
    for c in range(columns):
        wet_of = jnp.where(lane // levels == c, wet[c], wet_of)
    wet_mask = (lane % levels < wet_of).astype(F32)

    def tile_at(distance):
        slot, live = jnp.int32(0), jnp.int32(0)
        for k in range(slots):
            hit = jnp.logical_and(off[0, k] == distance * sign, k < cnt[0])
            slot = jnp.where(hit, k, slot)
            live = jnp.where(hit, 1, live)
        return slot, live.astype(F32)

    places = {d: tile_at(d) for d in (-2, 2, -1, 1, 0)}

    for load in loads[:4]:
        load.wait()
    per = LANES // levels
    flat = inv[...].reshape(boxes, levels)
    wide = jnp.concatenate([flat] * per, axis=1)
    row = lax.broadcasted_iota(jnp.int32, (boxes, LANES), 0)
    lanes = lax.broadcasted_iota(jnp.int32, (boxes, LANES), 1)
    wide = jnp.where((row // levels) % per == lanes // levels, wide, 0.0)
    blocks = []
    for b in range(boxes // LANES):
        span = slice(b * LANES, (b + 1) * LANES)
        high, low = halves(wide[span] * wet_mask[:, span])
        blocks.append(jnp.concatenate([high, low], axis=0))

    ident = (
        lax.broadcasted_iota(jnp.int32, (ntr, ntr), 0) == lax.broadcasted_iota(jnp.int32, (ntr, ntr), 1)
    ).astype(F32)
    own_rows = (
        lax.broadcasted_iota(jnp.int32, (tr, ntr), 0) + tracer * tr
        == lax.broadcasted_iota(jnp.int32, (tr, ntr), 1)
    ).astype(F32)
    highest = lax.Precision.HIGHEST
    uptake = halves(up[...])
    uptake_own = halves(
        lax.dot_general(own_rows, up[...], ROWS_DIM, precision=highest, preferred_element_type=F32)
    )
    release = halves(
        lax.dot_general(ident, rel[...], ROWS_DIM, precision=highest, preferred_element_type=F32)
    )

    def joined(ref, i):
        if tr % 8 == 0:
            return ref[i].reshape(ntr, boxes)
        return jnp.concatenate([ref[i, j] for j in range(tracers_n)], axis=0)

    def settle(a):
        high, low = halves(a)
        zero = jnp.zeros((tr, LANES), BF16)
        parts = []
        for b, block in enumerate(blocks):
            span = slice(b * LANES, (b + 1) * LANES)
            first = jnp.concatenate([high[:, span], high[:, span]], axis=1)
            second = jnp.concatenate([low[:, span], zero], axis=1)
            if tr % 16 == 0:
                both = dot(jnp.concatenate([first, second], axis=0), block)
                parts.append(both[:tr] + both[tr:])
            else:
                parts.append(dot(first, block) + dot(second, block))
        return jnp.concatenate(parts, axis=1)

    def make_gain(n):
        for j in peers:
            state_copy(n, j).wait_recv()
        pltpu.make_async_copy(states_hbm.at[n], full_state.at[n, tracer], own_sem.at[n]).wait()
        bent = jnp.tanh(dot_split(uptake, joined(full_state, n)))
        gain[...] = 1.0 - bent * bent

    def drain(i):
        for k in range(4):
            region_copy(i, k).wait_send()
        for j in peers:
            settled_copy(i, j).wait_send()
            state_copy(steps - 1 - i, j).wait_send()

    def step(i, first):
        n = steps - 1 - i
        settled = settle(adj[...])
        full_settled[i, tracer] = settled
        half = settled.astype(BF16)

        def term(distance):
            slot, live = places[distance]
            return dot(half, tiles[slot]) * live

        def send_settled():
            for j in peers:
                settled_copy(i, j).start()

        if first:
            loads[4].wait()
            relay_out[i] = term(-2)
            direct_out[i] = term(2)
            peer_out[i] = term(-1)
            merged_out[i] = term(1)
            total = term(0)
            pl.semaphore_wait(barrier, 4 + len(others))
            for j in peers:
                state_copy(n, j).start()
            send_settled()
            region_copy(i, 0).start()
            region_copy(i, 1).start()
            region_copy(i, 3).start()
            region_copy(i, 2).start()
            if steps > 1:
                for j in peers:
                    state_copy(n - 1, j).start()
        else:
            direct_out[i] = term(2)
            region_copy(i, 1).start()
            send_settled()
            relay_out[i] = term(-2)
            region_copy(i, 0).start()
            merged_out[i] = term(1)
            region_copy(i, 3).start()
            peer_out[i] = term(-1)
            region_copy(i, 2).start()
            total = term(0)

        @pl.when(n >= 2)
        def _():
            for j in peers:
                state_copy(n - 2, j).start()

        if not first:
            drain(i - 1)
        make_gain(n)
        for j in peers:
            settled_copy(i, j).wait_recv()
        weighted = gain[...] * dot_split(release, joined(full_settled, i))
        total = total + dot_split(uptake_own, weighted)

        region_copy(i, 2).wait_recv()
        total = total + peer_in[i]
        region_copy(i, 1).wait_recv()
        total = total + direct_in[i]
        region_copy(i, 3).wait_recv()
        total = total + merged_in[i]
        region_copy(i, 0).wait_recv()
        adj[...] = wet_mask * (total + relay_in[i])

    def later_step(i, carry):
        step(i, False)
        return carry

    step(0, True)
    lax.fori_loop(1, steps, later_step, 0)
    out[...] = adj[...]
    drain(steps - 1)


def local(
    cotangent,
    states,
    implicit_inverse,
    wet_levels,
    explicit_tiles,
    tile_offset,
    tile_count,
    uptake_weight,
    release_weight,
):
    tr, boxes = cotangent.shape
    steps = states.shape[0]
    tracers_n = lax.axis_size("tracer")
    ntr = tracers_n * tr
    slots = explicit_tiles.shape[1]
    peers = max(tracers_n - 1, 1)
    hbm = pl.BlockSpec(memory_space=pl.ANY)
    smem = pl.BlockSpec(memory_space=pltpu.SMEM)
    message = pltpu.VMEM((steps, tr, boxes), F32)
    gathered = pltpu.VMEM((steps, tracers_n, tr, boxes), F32)
    sems = pltpu.SemaphoreType.DMA
    return pl.pallas_call(
        kernel,
        out_shape=jax.ShapeDtypeStruct((tr, boxes), F32),
        in_specs=[hbm, hbm, hbm, smem, hbm, smem, smem, hbm, hbm],
        out_specs=pl.BlockSpec(memory_space=pltpu.VMEM),
        scratch_shapes=[
            pltpu.VMEM(explicit_tiles.shape[1:], BF16),
            pltpu.VMEM(implicit_inverse.shape, F32),
            pltpu.VMEM(uptake_weight.shape, F32),
            pltpu.VMEM(release_weight.shape, F32),
            pltpu.VMEM((tr, boxes), F32),
            gathered,
            gathered,
            pltpu.VMEM((ntr, boxes), F32),
        ]
        + [message] * 8
        + [
            sems((5,)),
            sems((steps,)),
            sems((steps, 4)),
            sems((steps, 4)),
            sems((steps, peers)),
            sems((steps, peers)),
            sems((steps, peers)),
            sems((steps, peers)),
        ],
        compiler_params=pltpu.CompilerParams(
            collective_id=0, has_side_effects=True, vmem_limit_bytes=60 * 1024 * 1024
        ),
        name="adjoint_steps",
    )(
        cotangent,
        states,
        implicit_inverse,
        wet_levels,
        explicit_tiles,
        tile_offset,
        tile_count,
        uptake_weight,
        release_weight,
    )


def solution(mesh):
    placed = (
        P("tracer", "region"),
        P(None, "tracer", "region"),
        P("region", None, None),
        P("region"),
        P("region", None, None, None),
        P("region", None),
        P("region"),
        P(),
        P(),
    )
    return jax.shard_map(
        local, mesh=mesh, in_specs=placed, out_specs=P("tracer", "region"), check_vma=False
    )
```
